128 devices in a mesh: rows: 32 (over y, x, core), cols: 4 (over z).
Axes of the slice: x: 4, y: 4, z: 4, core: 2. Of those that a mesh axis runs over, the one named last changes fastest.
Arguments:
- embeddings: bfloat16 [262144, 2048], P('rows', 'cols'), may hold values from -6 to 6
- pick_rows: int32 [2, 32], replicated, may hold values from 0 to 262143, as said below
Outputs:
- residual: float32 [262144, 2048], P('rows', 'cols')
The draws below stay inside these ranges and needn't reach their ends.
Inputs may be any that keep to these rules, and one draw needn't show every extreme that they name: `pick_rows`: all 64 indices are distinct; the picks of one round fall on the row owners as evenly as their count allows.
All inputs are finite; a program needn't handle non-finite values.
Results may differ from the reference program's by a relative error of at most 0.0003.
Values sent between devices are 32-bit elements; how exact they have to be, the bound alone decides.
No kernel may reach another device: no remote copies, remote signals or barrier semaphores. Data moves between devices by JAX's collectives and lax.ppermute only.
A program may use at most 128 MiB of HBM per device.

```python
import jax
import jax.numpy as jnp
from jax import lax

W = 2048
ROWS_DEV = 8192
PICKS = 32
ROUNDS = 2
NROWS = 262144


def draw_pick_rows(key, part):
    key = jax.random.fold_in(key, 7)
    owners_total = NROWS // ROWS_DEV
    half_rows = ROWS_DEV // 2
    result_list = []
    for round_index in range(ROUNDS):
        round_key = jax.random.fold_in(key, round_index)
        owner_key, offset_key = jax.random.split(round_key)
        shift_value = jax.random.randint(owner_key, (), 0, owners_total)
        owner_ids = (jnp.arange(PICKS, dtype=jnp.int32) + shift_value) % owners_total
        slot_order = jnp.arange(PICKS, dtype=jnp.int32) // owners_total
        offset_table = jax.random.permutation(offset_key, half_rows).astype(jnp.int32)
        local_ids = jnp.take(offset_table, (slot_order + owner_ids * 7) % half_rows) + round_index * half_rows
        result_list.append(owner_ids * ROWS_DEV + local_ids)
    return jnp.stack(result_list, axis=0).astype(jnp.int32)


def block_scale(key, shape, cuts, low, largest):
    loudness = 1.0
    for position, parts in cuts:
        steps = jax.random.uniform(jax.random.fold_in(jax.random.fold_in(key, 6), position), (parts,), jnp.float32, low / len(cuts), largest / len(cuts))
        loudness = loudness * jnp.repeat(jnp.exp(steps), shape[position] // parts).reshape((-1,) + (1,) * (len(shape) - 1 - position))
    return loudness


def noise(own_key, dims, spread, most, cuts=(), kind=jnp.bfloat16):
    drawn = spread * jax.random.normal(own_key, dims, jnp.float32)
    if cuts:
        drawn = drawn * block_scale(own_key, dims, cuts, -0.22, 0.18)
    return jnp.clip(drawn, -most, most).astype(kind)


def setup_inputs(seed: int = 0) -> dict:
    streams_of = jax.random.split(jax.random.key(seed), 3)
    return {
        "embeddings": noise(streams_of[0], (NROWS, W), 1.0, 6.0, ((0, 32), (1, 4))),
        "pick_rows": draw_pick_rows(jax.random.fold_in(streams_of[2], 71), 0),
    }


def orthonormal_panel(pick_panel):
    gram_matrix = jnp.dot(pick_panel.astype(jnp.float32), pick_panel.T.astype(jnp.float32), precision=lax.Precision.HIGHEST, preferred_element_type=jnp.float32)
    factor = jnp.linalg.cholesky(gram_matrix)
    return jax.scipy.linalg.solve_triangular(factor, pick_panel, lower=True)

def reference(embeddings, pick_rows):
    residual = embeddings.astype(jnp.float32)
    for round_index in range(ROUNDS):
        pick_panel = jnp.take(residual, pick_rows[round_index], axis=0)
        basis_rows = orthonormal_panel(pick_panel)
        weights = jnp.dot(residual.astype(jnp.float32), basis_rows.T.astype(jnp.float32), precision=lax.Precision.HIGHEST, preferred_element_type=jnp.float32)
        residual = residual - jnp.dot(weights.astype(jnp.float32), basis_rows.astype(jnp.float32), precision=lax.Precision.HIGHEST, preferred_element_type=jnp.float32)
    return residual
```

```python
import functools

import jax
import jax.numpy as jnp
from jax import lax
from jax.experimental import pallas as pl
from jax.experimental.pallas import tpu as pltpu
from jax.sharding import PartitionSpec as P

HIGH = lax.Precision.HIGHEST
CHUNKS = 2
VMEM_LIMIT = 48 * 1024 * 1024
F32, BF16 = jnp.float32, jnp.bfloat16


def whole():
    return pl.BlockSpec(memory_space=pltpu.VMEM)


def anywhere():
    return pl.BlockSpec(memory_space=pl.ANY)


def scalars():
    return pl.BlockSpec(memory_space=pltpu.SMEM)


def in_vmem(array):
    return pltpu.with_memory_space_constraint(array, pltpu.VMEM)


def call(body, out_shape, in_specs, out_specs, scratch=(), aliases=None, name=None):
    return pl.pallas_call(
        body,
        out_shape=out_shape,
        in_specs=in_specs,
        out_specs=out_specs,
        scratch_shapes=list(scratch),
        input_output_aliases=aliases or {},
        compiler_params=pltpu.CompilerParams(vmem_limit_bytes=VMEM_LIMIT),
        name=name,
    )


def own_picks(emb, pick_rows, copies):
    rows, width = emb.shape
    rounds, picks = pick_rows.shape
    tile = 16

    def body(picks_ref, emb_ref, out_ref, held, sems):
        first = lax.axis_index("rows") * rows
        offsets, moves = [], []
        for r in range(rounds):
            local = jnp.int32(0)
            for i in range(picks):
                at = picks_ref[r, i] - first
                local = local + jnp.where((at >= 0) & (at < rows), at, 0)
            base = pl.multiple_of((local // tile) * tile, tile)
            offsets.append(local - base)
            move = pltpu.make_async_copy(emb_ref.at[pl.ds(base, tile), :], held.at[r], sems.at[r])
            move.start()
            moves.append(move)
        for r in range(rounds):
            moves[r].wait()
            block = held[r].astype(F32)
            line = lax.broadcasted_iota(jnp.int32, (tile, width), 0)
            row = jnp.sum(jnp.where(line == offsets[r], block, 0.0), axis=0, keepdims=True)
            out_ref[:, r : r + 1, :] = jnp.broadcast_to(row[None], (copies, 1, width))

    return call(
        body,
        jax.ShapeDtypeStruct((copies, rounds, width), F32),
        [scalars(), anywhere()],
        whole(),
        [pltpu.VMEM((rounds, tile, width), BF16), pltpu.SemaphoreType.DMA((rounds,))],
        name="own_picks",
    )(pick_rows, emb)


def paired_panel(panel):
    panel = panel.astype(BF16)
    zero = jnp.zeros_like(panel)
    return jnp.concatenate(
        [jnp.concatenate([panel, zero], axis=1), jnp.concatenate([zero, panel], axis=1)], axis=0
    )


def paired_products(top, bottom, paired):
    both = jnp.concatenate([top, bottom], axis=1)
    return lax.dot_general(both, paired, (((1,), (1,)), ((), ())), preferred_element_type=F32)


def diagonal_products(emb, panel, block_rows):
    picks = panel.shape[0]
    group = block_rows // (2 * CHUNKS)
    half = group // 2

    def body(emb_ref, panel_ref, gram_ref, *out_refs):
        block = lax.rem(lax.axis_index("cols") + 2, 4)
        panel = panel_ref[...]
        paired = paired_panel(panel)
        low = panel.astype(BF16)
        gram_ref[...] = paired_products(low[: picks // 2], low[picks // 2 :], paired)
        for k in range(CHUNKS):
            base = pl.multiple_of(block * block_rows + k * 2 * group, 2 * group)
            got = paired_products(emb_ref[pl.ds(base, group), :], emb_ref[pl.ds(base + group, group), :], paired)
            out_refs[2 * k][...] = got[:half]
            out_refs[2 * k + 1][...] = got[half:]

    shapes = [pltpu.VMEM((picks // 2, 2 * picks), F32)] + [pltpu.VMEM((half, 2 * picks), F32)] * (2 * CHUNKS)
    return call(body, shapes, [whole(), whole()], [whole()] * len(shapes), name="diagonal_products")(
        in_vmem(emb), in_vmem(panel)
    )


def other_products(emb, panel, block_rows):
    picks = panel.shape[0]
    group = block_rows // (2 * CHUNKS)

    def body(emb_ref, panel_ref, *out_refs):
        me = lax.axis_index("cols")
        paired = paired_panel(panel_ref[...])
        for k in range(CHUNKS):
            for j, shift in enumerate((1, 3, 0)):
                block = lax.rem(me + shift, 4)
                base = pl.multiple_of(block * block_rows + k * 2 * group, 2 * group)
                out_refs[3 * k + j][...] = paired_products(
                    emb_ref[pl.ds(base, group), :], emb_ref[pl.ds(base + group, group), :], paired
                )

    shapes = [pltpu.VMEM((group, 2 * picks), F32)] * (3 * CHUNKS)
    return call(body, shapes, [whole(), whole()], [whole()] * len(shapes), name="other_products")(
        in_vmem(emb), in_vmem(panel)
    )


def split(value):
    high = value.astype(BF16)
    rest = value - high.astype(F32)
    middle = rest.astype(BF16)
    low = (rest - middle.astype(F32)).astype(BF16)
    return high, middle, low


def dot_full(a, b):
    return jnp.dot(a, b, precision=HIGH, preferred_element_type=F32)


def update_matrix(gram_parts, panel):
    picks, width = panel.shape

    def body(*refs):
        panel_ref, out_ref = refs[-2:]
        total = refs[0][...]
        for ref in refs[1:-2]:
            total = total + ref[...]
        gram = jnp.concatenate([total[:, :picks], total[:, picks:]], axis=0)
        lane = lax.broadcasted_iota(jnp.int32, gram.shape, 1)
        line = lax.broadcasted_iota(jnp.int32, gram.shape, 0)
        inverse = gram
        for k in range(picks):
            pivot = 1.0 / inverse[k : k + 1, k : k + 1]
            row = jnp.where(lane[:1] == k, pivot, inverse[k : k + 1, :] * pivot)
            column = inverse[:, k : k + 1]
            cleared = jnp.where(lane == k, 0.0, inverse)
            inverse = jnp.where(line == k, row, cleared - column * row)
        eye = jnp.where(lane == line, 1.0, 0.0)
        inverse = inverse + dot_full(inverse, eye - dot_full(gram, inverse))
        high, middle, low = split(dot_full(inverse, panel_ref[...]))
        out_ref[...] = jnp.concatenate([high, high, high, low, middle, middle], axis=0)

    return call(
        body,
        pltpu.VMEM((6 * picks, width), BF16),
        [whole()] * (len(gram_parts) + 1),
        whole(),
        name="update_matrix",
    )(*[in_vmem(g) for g in gram_parts], in_vmem(panel))


def update(emb, right, out, pieces, block_rows, name):
    rows, width = emb.shape
    picks = right.shape[0] // 6
    group = block_rows // (2 * CHUNKS)
    step = 256
    steps = [(n, g, t) for n, (p, *_) in enumerate(pieces) for g in range(2) for t in range(0, p.shape[0], min(step, p.shape[0]))]
    step = min(step, min(p.shape[0] for p, *_ in pieces))

    def body(*refs):
        emb_ref, right_ref = refs[:2]
        packed = refs[2 : 2 + len(pieces)]
        out_ref, staged, sems = refs[-3:]
        me = lax.axis_index("cols")
        right_mat = right_ref[...]
        lane = lax.broadcasted_iota(jnp.int32, (step, 2 * picks), 1)
        moves = []
        for i, (n, g, t) in enumerate(steps):
            _, shift, k, first = pieces[n]
            block = lax.rem(me + shift, 4)
            base = pl.multiple_of(block * block_rows + k * 2 * group + g * group + first + t, step)
            got = packed[n][t : t + step, :]
            high = got.astype(BF16).astype(F32)
            rest = got - high
            middle = rest.astype(BF16).astype(F32)
            low = rest - middle
            if g == 0:
                first_part = jnp.where(lane < picks, high, pltpu.roll(middle, picks, 1))
                second_part = jnp.where(lane < picks, low, pltpu.roll(high, picks, 1))
            else:
                first_part = jnp.where(lane < picks, pltpu.roll(high, picks, 1), middle)
                second_part = jnp.where(lane < picks, pltpu.roll(low, picks, 1), high)
            first_part = first_part.astype(BF16)
            left = jnp.concatenate([first_part, second_part.astype(BF16), first_part], axis=1)
            taken = jnp.dot(left, right_mat, preferred_element_type=F32)
            staged[i] = emb_ref[pl.ds(base, step), :].astype(F32) - taken
            move = pltpu.make_async_copy(staged.at[i], out_ref.at[pl.ds(base, step), :], sems.at[i])
            move.start()
            moves.append(move)
        for move in moves:
            move.wait()

    operands = [in_vmem(emb), in_vmem(right)] + [in_vmem(p) for p, *_ in pieces]
    specs = [whole()] * len(operands)
    aliases = None
    if out is not None:
        operands.append(out)
        specs.append(anywhere())
        aliases = {len(operands) - 1: 0}
    return call(
        body,
        jax.ShapeDtypeStruct((rows, width), F32),
        specs,
        anywhere(),
        [pltpu.VMEM((len(steps), step, width), F32), pltpu.SemaphoreType.DMA((len(steps),))],
        aliases,
        name=name,
    )(*operands)


def per_device(emb, pick_rows, owners):
    rows, width = emb.shape
    rounds = pick_rows.shape[0]
    block_rows = rows // 4
    half = block_rows // (4 * CHUNKS)

    def send(value, shift):
        return lax.ppermute(value, "cols", [(i, (i + shift) % 4) for i in range(4)])

    mine = own_picks(emb, pick_rows, owners)
    panel = lax.all_to_all(mine, "rows", 0, 0, tiled=True).reshape(owners * rounds, width)
    gram, *diag = diagonal_products(emb, panel, block_rows)
    from_prev, from_next = [], []
    for k in range(CHUNKS):
        up, down = diag[2 * k], diag[2 * k + 1]
        if k == 0:
            up, down = jnp.concatenate([up, gram]), jnp.concatenate([down, gram])
        from_prev.append(send(up, 1))
        from_next.append(send(down, -1))
    others = other_products(emb, panel, block_rows)
    gram_prev, gram_next = from_prev[0][half:], from_next[0][half:]
    got_prev, got_next = [], []
    for k in range(CHUNKS):
        to_next, to_prev = others[3 * k], others[3 * k + 1]
        up = [to_next[:half] + from_prev[k][:half], to_next[half:]]
        down = [to_prev[:half], to_prev[half:] + from_next[k][:half]]
        if k == 0:
            up.append(gram_prev)
        got_prev.append(send(jnp.concatenate(up), 1))
        got_next.append(send(jnp.concatenate(down), -1))
    right = update_matrix([gram, gram_prev, gram_next, got_prev[0][2 * half :]], panel)
    own, block_prev, block_next = [], [], []
    for k in range(CHUNKS):
        total = others[3 * k + 2] + got_prev[k][: 2 * half] + got_next[k]
        own.append(total)
        block_prev.append(send(total, 1))
        block_next.append(send(total, -1))
    across_top, across_bottom = [], []
    for k in range(CHUNKS):
        across_top.append(send(block_prev[k][:half], 1))
        across_bottom.append(send(block_next[k][half:], -1))
    out = None
    for k in range(CHUNKS):
        out = update(emb, right, out, [(own[k], 0, k, 0)], block_rows, "update_own")
    for k in range(CHUNKS):
        out = update(
            emb, right, out, [(block_prev[k], 3, k, 0), (block_next[k], 1, k, 0)], block_rows, "update_near"
        )
    for k in range(CHUNKS):
        out = update(
            emb, right, out, [(across_top[k], 2, k, 0), (across_bottom[k], 2, k, half)], block_rows, "update_across"
        )
    return out


def solution(mesh):
    return jax.shard_map(
        functools.partial(per_device, owners=mesh.shape["rows"]),
        mesh=mesh,
        in_specs=(P("rows", "cols"), P()),
        out_specs=P("rows", "cols"),
        check_vma=False,
    )
```

```python
import functools

import jax
import jax.numpy as jnp
from jax import lax
from jax.experimental import pallas as pl
from jax.experimental.pallas import tpu as pltpu
from jax.sharding import PartitionSpec as P

HIGH = lax.Precision.HIGHEST
CHUNKS = (512, 512)
VMEM_LIMIT = 16 * 1024 * 1024
F32, BF16 = jnp.float32, jnp.bfloat16


def whole():
    return pl.BlockSpec(memory_space=pltpu.VMEM)


def anywhere():
    return pl.BlockSpec(memory_space=pl.ANY)


def scalars():
    return pl.BlockSpec(memory_space=pltpu.SMEM)


def in_vmem(array):
    return pltpu.with_memory_space_constraint(array, pltpu.VMEM)


def in_hbm(array):
    return pltpu.with_memory_space_constraint(array, pltpu.HBM)


def in_hbm(array):
    return pltpu.with_memory_space_constraint(array, pltpu.HBM)


def call(body, out_shape, in_specs, out_specs, scratch=(), aliases=None, name=None, micros=1.0):
    return pl.pallas_call(
        body,
        out_shape=out_shape,
        in_specs=in_specs,
        out_specs=out_specs,
        scratch_shapes=list(scratch),
        input_output_aliases=aliases or {},
        compiler_params=pltpu.CompilerParams(vmem_limit_bytes=VMEM_LIMIT),
        cost_estimate=pl.CostEstimate(flops=0, bytes_accessed=int(micros * 3.0e6), transcendentals=0),
        name=name,
    )


def first_partner(core, place):
    return place ^ 1 if core == 0 else place ^ 3


def second_partner(core, place):
    return place ^ 3 if core == 0 else place ^ 1


def kept():
    place, odd = lax.axis_index("cols"), lax.rem(lax.axis_index("rows"), 2) == 1
    high, low = place // 2, lax.rem(place, 2)
    gray = lax.rem(high + low, 2)
    return jnp.where(odd, high, gray), jnp.where(odd, low, high), jnp.where(odd, 1 - low, high)


def tile_of(size):
    return max(s for s in range(16, 257, 16) if size % s == 0)


def block_start(half, quarter, block_rows, chunk):
    return (2 * half + quarter) * block_rows + 2 * sum(CHUNKS[:chunk])


def own_picks(emb, pick_rows, copies, block_rows):
    rows, width = emb.shape
    rounds, picks = pick_rows.shape
    tile, size = 16, 2 * CHUNKS[0]

    def body(picks_ref, emb_ref, out_ref, ahead_ref, table, held, sems, table_sem, ahead_sems):
        load = pltpu.make_async_copy(picks_ref, table, table_sem)
        load.start()
        half, _, quarter = kept()
        moves = []
        for j in range(2):
            base = block_start(1 - half, quarter if j else 1 - quarter, block_rows, 0)
            for g in range(2):
                at = g * (size // 2)
                moves.append(
                    pltpu.make_async_copy(
                        emb_ref.at[pl.ds(pl.multiple_of(base + at, 16), size // 2), :],
                        ahead_ref.at[j, pl.ds(at, size // 2), :],
                        ahead_sems.at[2 * j + g],
                    )
                )
        load.wait()
        first = lax.axis_index("rows") * rows
        offsets, found = [], []
        for r in range(rounds):
            local = jnp.int32(0)
            for i in range(picks):
                at = table[r, i] - first
                local = local + jnp.where((at >= 0) & (at < rows), at, 0)
            base = pl.multiple_of((local // tile) * tile, tile)
            offsets.append(local - base)
            move = pltpu.make_async_copy(emb_ref.at[pl.ds(base, tile), :], held.at[r], sems.at[r])
            move.start()
            found.append(move)
        for move in moves:
            move.start()
        for r in range(rounds):
            found[r].wait()
            block = held[r].astype(F32)
            line = lax.broadcasted_iota(jnp.int32, (tile, width), 0)
            row = jnp.sum(jnp.where(line == offsets[r], block, 0.0), axis=0, keepdims=True)
            out_ref[:, r : r + 1, :] = jnp.broadcast_to(row[None], (copies, 1, width))
        for move in moves:
            move.wait()

    return call(
        body,
        [pltpu.VMEM((copies, rounds, width), F32), pltpu.VMEM((2, size, width), BF16)],
        [anywhere(), anywhere()],
        [whole(), whole()],
        [
            pltpu.SMEM((rounds, picks), jnp.int32),
            pltpu.VMEM((rounds, tile, width), BF16),
            pltpu.SemaphoreType.DMA((rounds,)),
            pltpu.SemaphoreType.DMA,
            pltpu.SemaphoreType.DMA((4,)),
        ],
        name="own_picks",
    )(in_hbm(pick_rows), in_hbm(emb))


def paired_panel(panel):
    panel = panel.astype(BF16)
    zero = jnp.zeros_like(panel)
    return jnp.concatenate(
        [jnp.concatenate([panel, zero], axis=1), jnp.concatenate([zero, panel], axis=1)], axis=0
    )


def paired_products(top, bottom, paired):
    both = jnp.concatenate([top, bottom], axis=1)
    return lax.dot_general(both, paired, (((1,), (1,)), ((), ())), preferred_element_type=F32)


def given_first(ahead, panel):
    picks = panel.shape[0]
    size = CHUNKS[0]

    def body(ahead_ref, panel_ref, out_ref):
        panel = panel_ref[...]
        paired = paired_panel(panel)
        low = panel.astype(BF16)
        out_ref[2 * size :, :] = paired_products(low[: picks // 2], low[picks // 2 :], paired)
        for j in range(2):
            out_ref[j * size : (j + 1) * size, :] = paired_products(ahead_ref[j, :size, :], ahead_ref[j, size:, :], paired)

    return call(
        body, pltpu.VMEM((2 * size + picks // 2, 2 * picks), F32), [whole(), whole()], whole(), name="given_first"
    )(in_vmem(ahead), in_vmem(panel))


def quarter_products(emb_ref, start, size, paired):
    start = pl.multiple_of(start, 16)
    return paired_products(emb_ref[pl.ds(start, size), :], emb_ref[pl.ds(start + size, size), :], paired)


def given_rest(emb, panel, block_rows, chunks, after):
    picks = panel.shape[0]

    def body(emb_ref, panel_ref, _, *out_refs):
        half, _, quarter = kept()
        paired = paired_panel(panel_ref[...])
        for out_ref, k in zip(out_refs, chunks):
            size = CHUNKS[k]
            for j in range(2):
                start = block_start(1 - half, quarter if j else 1 - quarter, block_rows, k)
                out_ref[j * size : (j + 1) * size, :] = quarter_products(emb_ref, start, size, paired)

    shapes = [pltpu.VMEM((2 * CHUNKS[k], 2 * picks), F32) for k in chunks]
    return call(body, shapes, [whole(), whole(), anywhere()], [whole()] * len(shapes), name="given_rest")(
        emb, in_vmem(panel), after
    )


def kept_products(emb, panel, got, message, block_rows, k):
    picks = panel.shape[0]
    size = CHUNKS[k]
    extra = picks // 2 if k == 0 else 0

    def body(emb_ref, panel_ref, got_ref, mine_ref, out_ref, own_ref):
        half, quarter, _ = kept()
        paired = paired_panel(panel_ref[...])
        start = block_start(half, 1 - quarter, block_rows, k)
        out_ref[:size, :] = quarter_products(emb_ref, start, size, paired) + got_ref[:size, :]
        if extra:
            out_ref[size:, :] = got_ref[2 * size :, :] + mine_ref[2 * size :, :]
        start = block_start(half, quarter, block_rows, k)
        own_ref[...] = quarter_products(emb_ref, start, size, paired) + got_ref[size : 2 * size, :]

    return call(
        body,
        [pltpu.VMEM((size + extra, 2 * picks), F32), pltpu.VMEM((size, 2 * picks), F32)],
        [whole()] * 4,
        [whole()] * 2,
        name="kept_products",
    )(emb, in_vmem(panel), in_vmem(got), in_vmem(message))


def added(own, got, after):
    def body(own_ref, got_ref, *refs):
        refs[-1][...] = own_ref[...] + got_ref[: own.shape[0], :]

    return call(
        body, pltpu.VMEM(own.shape, F32), [whole(), whole()] + [anywhere()] * len(after), whole(), name="added"
    )(in_vmem(own), in_vmem(got), *after)


def stacked(top, bottom, after):
    def body(top_ref, bottom_ref, *refs):
        refs[-1][: top.shape[0], :] = top_ref[...]
        refs[-1][top.shape[0] :, :] = bottom_ref[...]

    return call(
        body,
        pltpu.VMEM((top.shape[0] + bottom.shape[0], top.shape[1]), F32),
        [whole(), whole()] + [anywhere()] * len(after),
        whole(),
        name="stacked",
    )(in_vmem(top), in_vmem(bottom), *after)


def split(value):
    high = value.astype(BF16)
    rest = value - high.astype(F32)
    middle = rest.astype(BF16)
    low = (rest - middle.astype(F32)).astype(BF16)
    return high, middle, low


def dot_full(a, b):
    return jnp.dot(a, b, precision=HIGH, preferred_element_type=F32)


def gram_of(sent_ref, got_ref):
    total = sent_ref[CHUNKS[0] :, :] + got_ref[CHUNKS[0] :, :]
    picks = total.shape[1] // 2
    return jnp.concatenate([total[:, :picks], total[:, picks:]], axis=0)


def inverted(matrix):
    lane = lax.broadcasted_iota(jnp.int32, matrix.shape, 1)
    line = lax.broadcasted_iota(jnp.int32, matrix.shape, 0)
    for k in range(0, matrix.shape[0], 2):
        first = jnp.broadcast_to(matrix[:, k : k + 1], matrix.shape)
        second = jnp.broadcast_to(matrix[:, k + 1 : k + 2], matrix.shape)
        a, b, d = first[k : k + 1], second[k : k + 1], second[k + 1 : k + 2]
        scale = 1.0 / (a * d - b * b)
        here, there = lane[:1] == k, lane[:1] == k + 1
        top = jnp.where(here, 1.0, jnp.where(there, 0.0, matrix[k : k + 1]))
        bottom = jnp.where(there, 1.0, jnp.where(here, 0.0, matrix[k + 1 : k + 2]))
        row = (d * top - b * bottom) * scale
        next_row = (a * bottom - b * top) * scale
        cleared = jnp.where((lane == k) | (lane == k + 1), 0.0, matrix)
        rest = cleared - first * row - second * next_row
        matrix = jnp.where(line == k, row, jnp.where(line == k + 1, next_row, rest))
    return matrix


def update_matrix(sent, got, panel):
    picks, width = panel.shape

    def body(sent_ref, got_ref, panel_ref, out_ref):
        gram = gram_of(sent_ref, got_ref)
        inverse = inverted(gram)
        lane = lax.broadcasted_iota(jnp.int32, gram.shape, 1)
        line = lax.broadcasted_iota(jnp.int32, gram.shape, 0)
        eye = jnp.where(lane == line, 1.0, 0.0)
        inverse = inverse + dot_full(inverse, eye - dot_full(gram, inverse))
        high, middle, low = split(dot_full(inverse, panel_ref[...]))
        out_ref[...] = jnp.concatenate([high, high, high, low, middle, middle], axis=0)

    return call(body, pltpu.VMEM((6 * picks, width), BF16), [whole()] * 3, whole(), name="update_matrix")(
        in_vmem(sent), in_vmem(got), in_vmem(panel)
    )


def update(emb, right, out, pieces, block_rows, name):
    rows, width = emb.shape
    picks = right.shape[0] // 6
    steps = []
    for n, (_, _, k, *_) in enumerate(pieces):
        size = CHUNKS[k]
        step = tile_of(size)
        steps += [(n, g, t, step) for g in range(2) for t in range(0, size, step)]
    biggest = max(s[3] for s in steps)
    count = len(pieces)

    def body(*refs):
        emb_ref, right_ref = refs[:2]
        out_ref, staged, sems = refs[-3:]
        half, quarter, partner_quarter = kept()
        right_mat = right_ref[...]
        moves = []
        for i, (n, g, t, step) in enumerate(steps):
            _, first, k, give, keeper = pieces[n]
            size = CHUNKS[k]
            own_half, own_quarter = (1 - half, partner_quarter) if give else (half, quarter)
            start = block_start(own_half, own_quarter if keeper else 1 - own_quarter, block_rows, k)
            base = pl.multiple_of(start + g * size + t, 16)
            got = refs[2 + n][first + t : first + t + step, :]
            lane = lax.broadcasted_iota(jnp.int32, (step, 2 * picks), 1)
            high = got.astype(BF16).astype(F32)
            rest = got - high
            middle = rest.astype(BF16).astype(F32)
            low = rest - middle
            if g == 0:
                first_part = jnp.where(lane < picks, high, pltpu.roll(middle, picks, 1))
                second_part = jnp.where(lane < picks, low, pltpu.roll(high, picks, 1))
            else:
                first_part = jnp.where(lane < picks, pltpu.roll(high, picks, 1), middle)
                second_part = jnp.where(lane < picks, pltpu.roll(low, picks, 1), high)
            first_part = first_part.astype(BF16)
            left = jnp.concatenate([first_part, second_part.astype(BF16), first_part], axis=1)
            taken = jnp.dot(left, right_mat, preferred_element_type=F32)
            staged[i, :step] = emb_ref[pl.ds(base, step), :].astype(F32) - taken
            move = pltpu.make_async_copy(staged.at[i, pl.ds(0, step)], out_ref.at[pl.ds(base, step), :], sems.at[i])
            move.start()
            moves.append(move)
        for move in moves:
            move.wait()

    operands = [emb, in_vmem(right)] + [in_vmem(p[0]) for p in pieces]
    specs = [whole()] * len(operands)
    aliases = None
    if out is not None:
        operands.append(out)
        specs.append(anywhere())
        aliases = {len(operands) - 1: 0}
    return call(
        body,
        jax.ShapeDtypeStruct((rows, width), F32),
        specs,
        anywhere(),
        [pltpu.VMEM((len(steps), biggest, width), F32), pltpu.SemaphoreType.DMA((len(steps),))],
        aliases,
        name=name,
    )(*operands)


def per_device(emb, pick_rows, owners):
    rows, width = emb.shape
    rounds = pick_rows.shape[0]
    block_rows = rows // 4
    count = len(CHUNKS)
    first_pairs = [(r * 4 + c, r * 4 + first_partner(r % 2, c)) for r in range(owners) for c in range(4)]
    second_pairs = [(r * 4 + c, r * 4 + second_partner(r % 2, c)) for r in range(owners) for c in range(4)]

    def swap_first(value):
        return lax.ppermute(value, ("rows", "cols"), first_pairs)

    def swap_second(value):
        return lax.ppermute(value, ("rows", "cols"), second_pairs)

    mine, ahead = own_picks(emb, pick_rows, owners, block_rows)
    panel = lax.all_to_all(mine, "rows", 0, 0, tiled=True).reshape(owners * rounds, width)

    messages = [given_first(ahead, panel)]
    messages += given_rest(emb, panel, block_rows, list(range(1, count)), messages[0])
    halves = [swap_first(m) for m in messages]
    sent, own = zip(*[kept_products(emb, panel, halves[k], messages[k], block_rows, k) for k in range(count)])
    quarters = [swap_second(m) for m in sent]
    right = update_matrix(sent[0], quarters[0], panel)

    totals, near, far = [], [], []
    for k in range(count):
        totals.append(added(own[k], quarters[k], [right] if k else []))
        near.append(swap_second(totals[k]))
    for k in range(count):
        far.append((swap_first(totals[k]), swap_first(near[k])))
    out = None
    for k in range(count):
        out = update(emb, right, out, [(totals[k], 0, k, False, True), (near[k], 0, k, False, False)], block_rows, "update_near")
    for k in range(count):
        pieces = [(far[k][0], 0, k, True, True), (far[k][1], 0, k, True, False)]
        out = update(emb, right, out, pieces, block_rows, "update_far")
    return out


def solution(mesh):
    return jax.shard_map(
        functools.partial(per_device, owners=mesh.shape["rows"]),
        mesh=mesh,
        in_specs=(P("rows", "cols"), P()),
        out_specs=P("rows", "cols"),
        check_vma=False,
    )
```

```python
import functools

import jax
import jax.numpy as jnp
from jax import lax
from jax.experimental import pallas as pl
from jax.experimental.pallas import tpu as pltpu
from jax.sharding import PartitionSpec as P

HIGH = lax.Precision.HIGHEST
CHUNKS = (512, 512)
VMEM_LIMIT = 16 * 1024 * 1024
F32, BF16 = jnp.float32, jnp.bfloat16


def whole():
    return pl.BlockSpec(memory_space=pltpu.VMEM)


def anywhere():
    return pl.BlockSpec(memory_space=pl.ANY)


def scalars():
    return pl.BlockSpec(memory_space=pltpu.SMEM)


def in_vmem(array):
    return pltpu.with_memory_space_constraint(array, pltpu.VMEM)


def in_hbm(array):
    return pltpu.with_memory_space_constraint(array, pltpu.HBM)


def in_hbm(array):
    return pltpu.with_memory_space_constraint(array, pltpu.HBM)


def call(body, out_shape, in_specs, out_specs, scratch=(), aliases=None, name=None, micros=1.0):
    return pl.pallas_call(
        body,
        out_shape=out_shape,
        in_specs=in_specs,
        out_specs=out_specs,
        scratch_shapes=list(scratch),
        input_output_aliases=aliases or {},
        compiler_params=pltpu.CompilerParams(vmem_limit_bytes=VMEM_LIMIT),
        cost_estimate=pl.CostEstimate(flops=0, bytes_accessed=int(micros * 3.0e6), transcendentals=0),
        name=name,
    )


def first_partner(core, place):
    return place ^ 1 if core == 0 else place ^ 3


def second_partner(core, place):
    return place ^ 3 if core == 0 else place ^ 1


def kept():
    place, odd = lax.axis_index("cols"), lax.rem(lax.axis_index("rows"), 2) == 1
    high, low = place // 2, lax.rem(place, 2)
    gray = lax.rem(high + low, 2)
    return jnp.where(odd, high, gray), jnp.where(odd, low, high), jnp.where(odd, 1 - low, high)


def tile_of(size):
    return max(s for s in range(16, 257, 16) if size % s == 0)


def block_start(half, quarter, block_rows, chunk):
    return (2 * half + quarter) * block_rows + 2 * sum(CHUNKS[:chunk])


def own_picks(emb, pick_rows, copies, block_rows):
    rows, width = emb.shape
    rounds, picks = pick_rows.shape
    tile, size = 16, 2 * CHUNKS[0]

    def body(picks_ref, emb_ref, out_ref, ahead_ref, table, held, sems, table_sem, ahead_sems):
        load = pltpu.make_async_copy(picks_ref, table, table_sem)
        load.start()
        half, _, quarter = kept()
        moves = []
        for j in range(2):
            base = block_start(1 - half, quarter if j else 1 - quarter, block_rows, 0)
            for g in range(2):
                at = g * (size // 2)
                moves.append(
                    pltpu.make_async_copy(
                        emb_ref.at[pl.ds(pl.multiple_of(base + at, 16), size // 2), :],
                        ahead_ref.at[j, pl.ds(at, size // 2), :],
                        ahead_sems.at[2 * j + g],
                    )
                )
        for move in moves:
            move.start()
        load.wait()
        first = lax.axis_index("rows") * rows
        offsets, found = [], []
        for r in range(rounds):
            local = jnp.int32(0)
            for i in range(picks):
                at = table[r, i] - first
                local = local + jnp.where((at >= 0) & (at < rows), at, 0)
            base = pl.multiple_of((local // tile) * tile, tile)
            offsets.append(local - base)
            move = pltpu.make_async_copy(emb_ref.at[pl.ds(base, tile), :], held.at[r], sems.at[r])
            move.start()
            found.append(move)
        for r in range(rounds):
            found[r].wait()
            block = held[r].astype(F32)
            line = lax.broadcasted_iota(jnp.int32, (tile, width), 0)
            row = jnp.sum(jnp.where(line == offsets[r], block, 0.0), axis=0, keepdims=True)
            out_ref[:, r : r + 1, :] = jnp.broadcast_to(row[None], (copies, 1, width))
        for move in moves:
            move.wait()

    return call(
        body,
        [pltpu.VMEM((copies, rounds, width), F32), pltpu.VMEM((2, size, width), BF16)],
        [anywhere(), anywhere()],
        [whole(), whole()],
        [
            pltpu.SMEM((rounds, picks), jnp.int32),
            pltpu.VMEM((rounds, tile, width), BF16),
            pltpu.SemaphoreType.DMA((rounds,)),
            pltpu.SemaphoreType.DMA,
            pltpu.SemaphoreType.DMA((4,)),
        ],
        name="own_picks",
    )(in_hbm(pick_rows), in_hbm(emb))


def paired_panel(panel):
    panel = panel.astype(BF16)
    zero = jnp.zeros_like(panel)
    return jnp.concatenate(
        [jnp.concatenate([panel, zero], axis=1), jnp.concatenate([zero, panel], axis=1)], axis=0
    )


def paired_products(top, bottom, paired):
    both = jnp.concatenate([top, bottom], axis=1)
    return lax.dot_general(both, paired, (((1,), (1,)), ((), ())), preferred_element_type=F32)


def given_first(ahead, panel):
    picks = panel.shape[0]
    size = CHUNKS[0]

    def body(ahead_ref, panel_ref, out_ref):
        panel = panel_ref[...]
        paired = paired_panel(panel)
        low = panel.astype(BF16)
        out_ref[2 * size :, :] = paired_products(low[: picks // 2], low[picks // 2 :], paired)
        for j in range(2):
            out_ref[j * size : (j + 1) * size, :] = paired_products(ahead_ref[j, :size, :], ahead_ref[j, size:, :], paired)

    return call(
        body, pltpu.VMEM((2 * size + picks // 2, 2 * picks), F32), [whole(), whole()], whole(), name="given_first"
    )(in_vmem(ahead), in_vmem(panel))


def quarter_products(emb_ref, start, size, paired):
    start = pl.multiple_of(start, 16)
    return paired_products(emb_ref[pl.ds(start, size), :], emb_ref[pl.ds(start + size, size), :], paired)


def given_rest(emb, panel, block_rows, k, after):
    picks = panel.shape[0]
    size = CHUNKS[k]

    def body(emb_ref, panel_ref, _, pass_ref, own_ref):
        half, _, quarter = kept()
        paired = paired_panel(panel_ref[...])
        pass_ref[...] = quarter_products(emb_ref, block_start(1 - half, 1 - quarter, block_rows, k), size, paired)
        own_ref[...] = quarter_products(emb_ref, block_start(1 - half, quarter, block_rows, k), size, paired)

    return call(
        body,
        [pltpu.VMEM((size, 2 * picks), F32)] * 2,
        [whole(), whole(), anywhere()],
        [whole()] * 2,
        name="given_rest",
    )(emb, in_vmem(panel), after)


def kept_products(emb, panel, got, message, block_rows, k):
    picks = panel.shape[0]
    size = CHUNKS[k]
    extra = picks // 2 if k == 0 else 0

    def body(emb_ref, panel_ref, got_ref, mine_ref, out_ref, own_ref):
        half, quarter, _ = kept()
        paired = paired_panel(panel_ref[...])
        start = block_start(half, 1 - quarter, block_rows, k)
        out_ref[:size, :] = quarter_products(emb_ref, start, size, paired) + got_ref[:size, :]
        if extra:
            out_ref[size:, :] = got_ref[2 * size :, :] + mine_ref[2 * size :, :]
        own = quarter_products(emb_ref, block_start(half, quarter, block_rows, k), size, paired)
        own_ref[...] = own + got_ref[size : 2 * size, :] if extra else own

    return call(
        body,
        [pltpu.VMEM((size + extra, 2 * picks), F32), pltpu.VMEM((size, 2 * picks), F32)],
        [whole()] * 4,
        [whole()] * 2,
        name="kept_products",
    )(emb, in_vmem(panel), in_vmem(got), in_vmem(message))


def added(parts, after):
    shape = parts[0].shape

    def body(*refs):
        total = refs[0][...]
        for ref in refs[1 : len(parts)]:
            total = total + ref[: shape[0], :]
        refs[-1][...] = total

    count = len(parts) + len(after)
    return call(body, pltpu.VMEM(shape, F32), [whole()] * count, whole(), name="added")(
        *[in_vmem(p) for p in parts], *[in_vmem(a) for a in after]
    )


def in_order(value, *after):
    def body(*refs):
        pass

    return call(
        body,
        pltpu.VMEM(value.shape, F32),
        [whole()] * (1 + len(after)),
        whole(),
        aliases={len(after): 0},
        name="in_order",
    )(*[in_vmem(a) for a in after], in_vmem(value))


def split(value):
    high = value.astype(BF16)
    rest = value - high.astype(F32)
    middle = rest.astype(BF16)
    low = (rest - middle.astype(F32)).astype(BF16)
    return high, middle, low


def dot_full(a, b):
    return jnp.dot(a, b, precision=HIGH, preferred_element_type=F32)


def gram_of(sent_ref, got_ref):
    total = sent_ref[CHUNKS[0] :, :] + got_ref[CHUNKS[0] :, :]
    picks = total.shape[1] // 2
    return jnp.concatenate([total[:, :picks], total[:, picks:]], axis=0)


def inverted(matrix):
    lane = lax.broadcasted_iota(jnp.int32, matrix.shape, 1)
    line = lax.broadcasted_iota(jnp.int32, matrix.shape, 0)
    for k in range(0, matrix.shape[0], 2):
        first = jnp.broadcast_to(matrix[:, k : k + 1], matrix.shape)
        second = jnp.broadcast_to(matrix[:, k + 1 : k + 2], matrix.shape)
        a, b, d = first[k : k + 1], second[k : k + 1], second[k + 1 : k + 2]
        scale = 1.0 / (a * d - b * b)
        here, there = lane[:1] == k, lane[:1] == k + 1
        top = jnp.where(here, 1.0, jnp.where(there, 0.0, matrix[k : k + 1]))
        bottom = jnp.where(there, 1.0, jnp.where(here, 0.0, matrix[k + 1 : k + 2]))
        row = (d * top - b * bottom) * scale
        next_row = (a * bottom - b * top) * scale
        cleared = jnp.where((lane == k) | (lane == k + 1), 0.0, matrix)
        rest = cleared - first * row - second * next_row
        matrix = jnp.where(line == k, row, jnp.where(line == k + 1, next_row, rest))
    return matrix


def update_matrix(sent, got, panel):
    picks, width = panel.shape

    def body(sent_ref, got_ref, panel_ref, out_ref):
        gram = gram_of(sent_ref, got_ref)
        inverse = inverted(gram)
        lane = lax.broadcasted_iota(jnp.int32, gram.shape, 1)
        line = lax.broadcasted_iota(jnp.int32, gram.shape, 0)
        eye = jnp.where(lane == line, 1.0, 0.0)
        inverse = inverse + dot_full(inverse, eye - dot_full(gram, inverse))
        high, middle, low = split(dot_full(inverse, panel_ref[...]))
        out_ref[...] = jnp.concatenate([high, high, high, low, middle, middle], axis=0)

    return call(body, pltpu.VMEM((6 * picks, width), BF16), [whole()] * 3, whole(), name="update_matrix")(
        in_vmem(sent), in_vmem(got), in_vmem(panel)
    )


def update(emb, right, out, pieces, block_rows, name, token=False):
    rows, width = emb.shape
    picks = right.shape[0] // 6
    steps = []
    for n, (_, _, k, *_) in enumerate(pieces):
        size = CHUNKS[k]
        step = tile_of(size)
        steps += [(n, g, t, step) for g in range(2) for t in range(0, size, step)]
    biggest = max(s[3] for s in steps)
    count = len(pieces)

    def body(*refs):
        emb_ref, right_ref = refs[:2]
        staged, sems = refs[-2:]
        out_ref = refs[-4 if token else -3]
        if token:
            refs[-3][...] = jnp.zeros_like(refs[-3])
        half, quarter, partner_quarter = kept()
        right_mat = right_ref[...]
        moves = []
        for i, (n, g, t, step) in enumerate(steps):
            _, first, k, give, keeper = pieces[n]
            size = CHUNKS[k]
            own_half, own_quarter = (1 - half, partner_quarter) if give else (half, quarter)
            start = block_start(own_half, own_quarter if keeper else 1 - own_quarter, block_rows, k)
            base = pl.multiple_of(start + g * size + t, 16)
            got = refs[2 + n][first + t : first + t + step, :]
            lane = lax.broadcasted_iota(jnp.int32, (step, 2 * picks), 1)
            high = got.astype(BF16).astype(F32)
            rest = got - high
            middle = rest.astype(BF16).astype(F32)
            low = rest - middle
            if g == 0:
                first_part = jnp.where(lane < picks, high, pltpu.roll(middle, picks, 1))
                second_part = jnp.where(lane < picks, low, pltpu.roll(high, picks, 1))
            else:
                first_part = jnp.where(lane < picks, pltpu.roll(high, picks, 1), middle)
                second_part = jnp.where(lane < picks, pltpu.roll(low, picks, 1), high)
            first_part = first_part.astype(BF16)
            left = jnp.concatenate([first_part, second_part.astype(BF16), first_part], axis=1)
            taken = jnp.dot(left, right_mat, preferred_element_type=F32)
            staged[i, :step] = emb_ref[pl.ds(base, step), :].astype(F32) - taken
            move = pltpu.make_async_copy(staged.at[i, pl.ds(0, step)], out_ref.at[pl.ds(base, step), :], sems.at[i])
            move.start()
            moves.append(move)
        for move in moves:
            move.wait()

    operands = [emb, in_vmem(right)] + [in_vmem(p[0]) for p in pieces]
    specs = [whole()] * len(operands)
    aliases = None
    if out is not None:
        operands.append(out)
        specs.append(anywhere())
        aliases = {len(operands) - 1: 0}
    return call(
        body,
        [jax.ShapeDtypeStruct((rows, width), F32)] + [pltpu.VMEM((8, 128), F32)] * token,
        specs,
        [anywhere()] + [whole()] * token,
        [pltpu.VMEM((len(steps), biggest, width), F32), pltpu.SemaphoreType.DMA((len(steps),))],
        aliases,
        name=name,
    )(*operands)


def per_device(emb, pick_rows, owners):
    rows, width = emb.shape
    rounds = pick_rows.shape[0]
    block_rows = rows // 4
    count = len(CHUNKS)
    first_pairs = [(r * 4 + c, r * 4 + first_partner(r % 2, c)) for r in range(owners) for c in range(4)]
    second_pairs = [(r * 4 + c, r * 4 + second_partner(r % 2, c)) for r in range(owners) for c in range(4)]

    def swap_first(value):
        return lax.ppermute(value, ("rows", "cols"), first_pairs)

    def swap_second(value):
        return lax.ppermute(value, ("rows", "cols"), second_pairs)

    mine, ahead = own_picks(emb, pick_rows, owners, block_rows)
    panel = lax.all_to_all(mine, "rows", 0, 0, tiled=True).reshape(owners * rounds, width)

    message = given_first(ahead, panel)
    got = swap_first(message)
    passing, staying = given_rest(emb, panel, block_rows, 1, message)
    next_got, staying = swap_first(passing), swap_first(staying)
    sent, own = zip(
        kept_products(emb, panel, got, message, block_rows, 0), kept_products(emb, panel, next_got, passing, block_rows, 1)
    )
    quarters = [swap_second(m) for m in sent]
    right = update_matrix(sent[0], quarters[0], panel)

    totals = [added([own[0], quarters[0]], [staying]), added([own[1], staying, quarters[1]], [right])]
    near = [swap_second(t) for t in totals]
    theirs = [swap_first(t) for t in totals]
    last = count - 1
    across = []
    for k in range(last):
        near[k] = in_order(near[k], theirs[k])
        across.append(swap_first(near[k]))
    pieces = [(totals[k], 0, k, False, True) for k in range(count)]
    pieces += [(near[k], 0, k, False, False) for k in range(last)]
    out, token = update(emb, right, None, pieces, block_rows, "update_near", True)
    near[last] = in_order(near[last], token)
    across.append(swap_first(near[last]))
    pieces = [(near[last], 0, last, False, False)]
    pieces += [(theirs[k], 0, k, True, True) for k in range(count)]
    pieces += [(across[k], 0, k, True, False) for k in range(last)]
    (out,) = update(emb, right, out, pieces, block_rows, "update_far")
    (out,) = update(emb, right, out, [(across[last], 0, last, True, False)], block_rows, "update_last")
    return out


def solution(mesh):
    return jax.shard_map(
        functools.partial(per_device, owners=mesh.shape["rows"]),
        mesh=mesh,
        in_specs=(P("rows", "cols"), P()),
        out_specs=P("rows", "cols"),
        check_vma=False,
    )
```

```python
import functools

import jax
import jax.numpy as jnp
from jax import lax
from jax.experimental import pallas as pl
from jax.experimental.pallas import tpu as pltpu
from jax.sharding import PartitionSpec as P

HIGH = lax.Precision.HIGHEST
CHUNKS = (512, 512)
VMEM_LIMIT = 16 * 1024 * 1024
F32, BF16 = jnp.float32, jnp.bfloat16


def whole():
    return pl.BlockSpec(memory_space=pltpu.VMEM)


def anywhere():
    return pl.BlockSpec(memory_space=pl.ANY)


def scalars():
    return pl.BlockSpec(memory_space=pltpu.SMEM)


def in_vmem(array):
    return pltpu.with_memory_space_constraint(array, pltpu.VMEM)


def in_hbm(array):
    return pltpu.with_memory_space_constraint(array, pltpu.HBM)


def in_hbm(array):
    return pltpu.with_memory_space_constraint(array, pltpu.HBM)


def call(body, out_shape, in_specs, out_specs, scratch=(), aliases=None, name=None, micros=1.0):
    return pl.pallas_call(
        body,
        out_shape=out_shape,
        in_specs=in_specs,
        out_specs=out_specs,
        scratch_shapes=list(scratch),
        input_output_aliases=aliases or {},
        compiler_params=pltpu.CompilerParams(vmem_limit_bytes=VMEM_LIMIT),
        cost_estimate=pl.CostEstimate(flops=0, bytes_accessed=int(micros * 3.0e6), transcendentals=0),
        name=name,
    )


def first_partner(core, place):
    return place ^ 1 if core == 0 else place ^ 3


def second_partner(core, place):
    return place ^ 3 if core == 0 else place ^ 1


def kept():
    place, odd = lax.axis_index("cols"), lax.rem(lax.axis_index("rows"), 2) == 1
    high, low = place // 2, lax.rem(place, 2)
    gray = lax.rem(high + low, 2)
    return jnp.where(odd, high, gray), jnp.where(odd, low, high), jnp.where(odd, 1 - low, high)


def tile_of(size):
    return max(s for s in range(16, 257, 16) if size % s == 0)


def block_start(half, quarter, block_rows, chunk):
    return (2 * half + quarter) * block_rows + 2 * sum(CHUNKS[:chunk])


def own_picks(emb, pick_rows, copies, block_rows):
    rows, width = emb.shape
    rounds, picks = pick_rows.shape
    tile, size = 16, 2 * CHUNKS[0]

    def body(picks_ref, emb_ref, out_ref, ahead_ref, table, held, sems, table_sem, ahead_sems):
        load = pltpu.make_async_copy(picks_ref, table, table_sem)
        load.start()
        half, _, quarter = kept()
        moves = []
        for j in range(2):
            base = block_start(1 - half, quarter if j else 1 - quarter, block_rows, 0)
            for g in range(2):
                at = g * (size // 2)
                moves.append(
                    pltpu.make_async_copy(
                        emb_ref.at[pl.ds(pl.multiple_of(base + at, 16), size // 2), :],
                        ahead_ref.at[j, pl.ds(at, size // 2), :],
                        ahead_sems.at[2 * j + g],
                    )
                )
        for move in moves:
            move.start()
        load.wait()
        first = lax.axis_index("rows") * rows
        offsets, found = [], []
        for r in range(rounds):
            local = jnp.int32(0)
            for i in range(picks):
                at = table[r, i] - first
                local = local + jnp.where((at >= 0) & (at < rows), at, 0)
            base = pl.multiple_of((local // tile) * tile, tile)
            offsets.append(local - base)
            move = pltpu.make_async_copy(emb_ref.at[pl.ds(base, tile), :], held.at[r], sems.at[r])
            move.start()
            found.append(move)
        for r in range(rounds):
            found[r].wait()
            block = held[r].astype(F32)
            line = lax.broadcasted_iota(jnp.int32, (tile, width), 0)
            row = jnp.sum(jnp.where(line == offsets[r], block, 0.0), axis=0, keepdims=True)
            out_ref[:, r : r + 1, :] = jnp.broadcast_to(row[None], (copies, 1, width))
        for move in moves:
            move.wait()

    return call(
        body,
        [pltpu.VMEM((copies, rounds, width), F32), pltpu.VMEM((2, size, width), BF16)],
        [anywhere(), anywhere()],
        [whole(), whole()],
        [
            pltpu.SMEM((rounds, picks), jnp.int32),
            pltpu.VMEM((rounds, tile, width), BF16),
            pltpu.SemaphoreType.DMA((rounds,)),
            pltpu.SemaphoreType.DMA,
            pltpu.SemaphoreType.DMA((4,)),
        ],
        name="own_picks",
    )(in_hbm(pick_rows), in_hbm(emb))


def paired_panel(panel):
    panel = panel.astype(BF16)
    zero = jnp.zeros_like(panel)
    return jnp.concatenate(
        [jnp.concatenate([panel, zero], axis=1), jnp.concatenate([zero, panel], axis=1)], axis=0
    )


def paired_products(top, bottom, paired):
    both = jnp.concatenate([top, bottom], axis=1)
    return lax.dot_general(both, paired, (((1,), (1,)), ((), ())), preferred_element_type=F32)


def given_first(ahead, panel):
    picks = panel.shape[0]
    size = CHUNKS[0]

    def body(ahead_ref, panel_ref, out_ref):
        panel = panel_ref[...]
        paired = paired_panel(panel)
        low = panel.astype(BF16)
        out_ref[2 * size :, :] = paired_products(low[: picks // 2], low[picks // 2 :], paired)
        for j in range(2):
            out_ref[j * size : (j + 1) * size, :] = paired_products(ahead_ref[j, :size, :], ahead_ref[j, size:, :], paired)

    return call(
        body, pltpu.VMEM((2 * size + picks // 2, 2 * picks), F32), [whole(), whole()], whole(), name="given_first"
    )(in_vmem(ahead), in_vmem(panel))


def quarter_products(emb_ref, start, size, paired):
    start = pl.multiple_of(start, 16)
    return paired_products(emb_ref[pl.ds(start, size), :], emb_ref[pl.ds(start + size, size), :], paired)


def given_rest(emb, panel, block_rows, k, after):
    picks = panel.shape[0]
    size = CHUNKS[k]

    def body(emb_ref, panel_ref, _, pass_ref, own_ref):
        half, _, quarter = kept()
        paired = paired_panel(panel_ref[...])
        pass_ref[...] = quarter_products(emb_ref, block_start(1 - half, 1 - quarter, block_rows, k), size, paired)
        own_ref[...] = quarter_products(emb_ref, block_start(1 - half, quarter, block_rows, k), size, paired)

    return call(
        body,
        [pltpu.VMEM((size, 2 * picks), F32)] * 2,
        [whole(), whole(), anywhere()],
        [whole()] * 2,
        name="given_rest",
    )(emb, in_vmem(panel), after)


def kept_products(emb, panel, got, message, block_rows, k):
    picks = panel.shape[0]
    size = CHUNKS[k]
    extra = picks // 2 if k == 0 else 0

    def body(emb_ref, panel_ref, got_ref, mine_ref, out_ref, own_ref):
        half, quarter, _ = kept()
        paired = paired_panel(panel_ref[...])
        start = block_start(half, 1 - quarter, block_rows, k)
        out_ref[:size, :] = quarter_products(emb_ref, start, size, paired) + got_ref[:size, :]
        if extra:
            out_ref[size:, :] = got_ref[2 * size :, :] + mine_ref[2 * size :, :]
        own = quarter_products(emb_ref, block_start(half, quarter, block_rows, k), size, paired)
        own_ref[...] = own + got_ref[size : 2 * size, :] if extra else own

    return call(
        body,
        [pltpu.VMEM((size + extra, 2 * picks), F32), pltpu.VMEM((size, 2 * picks), F32)],
        [whole()] * 4,
        [whole()] * 2,
        name="kept_products",
    )(emb, in_vmem(panel), in_vmem(got), in_vmem(message))


def added(parts, after):
    shape = parts[0].shape

    def body(*refs):
        total = refs[0][...]
        for ref in refs[1 : len(parts)]:
            total = total + ref[: shape[0], :]
        refs[-1][...] = total

    count = len(parts) + len(after)
    return call(body, pltpu.VMEM(shape, F32), [whole()] * count, whole(), name="added")(
        *[in_vmem(p) for p in parts], *[in_vmem(a) for a in after]
    )


def in_order(value, *after):
    def body(*refs):
        pass

    return call(
        body,
        pltpu.VMEM(value.shape, F32),
        [whole()] * (1 + len(after)),
        whole(),
        aliases={len(after): 0},
        name="in_order",
    )(*[in_vmem(a) for a in after], in_vmem(value))


def split(value):
    high = value.astype(BF16)
    rest = value - high.astype(F32)
    middle = rest.astype(BF16)
    low = (rest - middle.astype(F32)).astype(BF16)
    return high, middle, low


def dot_full(a, b):
    return jnp.dot(a, b, precision=HIGH, preferred_element_type=F32)


def gram_of(sent_ref, got_ref):
    total = sent_ref[CHUNKS[0] :, :] + got_ref[CHUNKS[0] :, :]
    picks = total.shape[1] // 2
    return jnp.concatenate([total[:, :picks], total[:, picks:]], axis=0)


def inverted(matrix):
    lane = lax.broadcasted_iota(jnp.int32, matrix.shape, 1)
    line = lax.broadcasted_iota(jnp.int32, matrix.shape, 0)
    for k in range(0, matrix.shape[0], 2):
        first = jnp.broadcast_to(matrix[:, k : k + 1], matrix.shape)
        second = jnp.broadcast_to(matrix[:, k + 1 : k + 2], matrix.shape)
        a, b, d = first[k : k + 1], second[k : k + 1], second[k + 1 : k + 2]
        scale = 1.0 / (a * d - b * b)
        here, there = lane[:1] == k, lane[:1] == k + 1
        top = jnp.where(here, 1.0, jnp.where(there, 0.0, matrix[k : k + 1]))
        bottom = jnp.where(there, 1.0, jnp.where(here, 0.0, matrix[k + 1 : k + 2]))
        row = (d * top - b * bottom) * scale
        next_row = (a * bottom - b * top) * scale
        cleared = jnp.where((lane == k) | (lane == k + 1), 0.0, matrix)
        rest = cleared - first * row - second * next_row
        matrix = jnp.where(line == k, row, jnp.where(line == k + 1, next_row, rest))
    return matrix


def update_matrix(sent, got, panel):
    picks, width = panel.shape

    def body(sent_ref, got_ref, panel_ref, out_ref):
        gram = gram_of(sent_ref, got_ref)
        inverse = inverted(gram)
        lane = lax.broadcasted_iota(jnp.int32, gram.shape, 1)
        line = lax.broadcasted_iota(jnp.int32, gram.shape, 0)
        eye = jnp.where(lane == line, 1.0, 0.0)
        inverse = inverse + dot_full(inverse, eye - dot_full(gram, inverse))
        high, middle, low = split(dot_full(inverse, panel_ref[...]))
        out_ref[...] = jnp.concatenate([high, high, high, low, middle, middle], axis=0)

    return call(body, pltpu.VMEM((6 * picks, width), BF16), [whole()] * 3, whole(), name="update_matrix")(
        in_vmem(sent), in_vmem(got), in_vmem(panel)
    )


def update(emb, right, out, pieces, block_rows, name, token=False):
    rows, width = emb.shape
    picks = right.shape[0] // 6
    steps = []
    for n, (_, _, k, *_) in enumerate(pieces):
        size = CHUNKS[k]
        step = tile_of(size)
        steps += [(n, g, t, step) for g in range(2) for t in range(0, size, step)]
    biggest = max(s[3] for s in steps)
    count = len(pieces)

    def body(*refs):
        emb_ref, right_ref = refs[:2]
        staged, sems = refs[-2:]
        out_ref = refs[-4 if token else -3]
        if token:
            refs[-3][...] = jnp.zeros_like(refs[-3])
        half, quarter, partner_quarter = kept()
        right_mat = right_ref[...]
        moves = []
        for i, (n, g, t, step) in enumerate(steps):
            _, first, k, give, keeper = pieces[n]
            size = CHUNKS[k]
            own_half, own_quarter = (1 - half, partner_quarter) if give else (half, quarter)
            start = block_start(own_half, own_quarter if keeper else 1 - own_quarter, block_rows, k)
            base = pl.multiple_of(start + g * size + t, 16)
            got = refs[2 + n][first + t : first + t + step, :]
            lane = lax.broadcasted_iota(jnp.int32, (step, 2 * picks), 1)
            high = got.astype(BF16).astype(F32)
            rest = got - high
            middle = rest.astype(BF16).astype(F32)
            low = rest - middle
            if g == 0:
                first_part = jnp.where(lane < picks, high, pltpu.roll(middle, picks, 1))
                second_part = jnp.where(lane < picks, low, pltpu.roll(high, picks, 1))
            else:
                first_part = jnp.where(lane < picks, pltpu.roll(high, picks, 1), middle)
                second_part = jnp.where(lane < picks, pltpu.roll(low, picks, 1), high)
            first_part = first_part.astype(BF16)
            left = jnp.concatenate([first_part, second_part.astype(BF16), first_part], axis=1)
            taken = jnp.dot(left, right_mat, preferred_element_type=F32)
            staged[i, :step] = emb_ref[pl.ds(base, step), :].astype(F32) - taken
            move = pltpu.make_async_copy(staged.at[i, pl.ds(0, step)], out_ref.at[pl.ds(base, step), :], sems.at[i])
            move.start()
            moves.append(move)
        for move in moves:
            move.wait()

    operands = [emb, in_vmem(right)] + [in_vmem(p[0]) for p in pieces]
    specs = [whole()] * len(operands)
    aliases = None
    if out is not None:
        operands.append(out)
        specs.append(anywhere())
        aliases = {len(operands) - 1: 0}
    return call(
        body,
        [jax.ShapeDtypeStruct((rows, width), F32)] + [pltpu.VMEM((8, 128), F32)] * token,
        specs,
        [anywhere()] + [whole()] * token,
        [pltpu.VMEM((len(steps), biggest, width), F32), pltpu.SemaphoreType.DMA((len(steps),))],
        aliases,
        name=name,
    )(*operands)


def per_device(emb, pick_rows, owners):
    rows, width = emb.shape
    rounds = pick_rows.shape[0]
    block_rows = rows // 4
    count = len(CHUNKS)
    first_pairs = [(r * 4 + c, r * 4 + first_partner(r % 2, c)) for r in range(owners) for c in range(4)]
    second_pairs = [(r * 4 + c, r * 4 + second_partner(r % 2, c)) for r in range(owners) for c in range(4)]

    def swap_first(value):
        return lax.ppermute(value, ("rows", "cols"), first_pairs)

    def swap_second(value):
        return lax.ppermute(value, ("rows", "cols"), second_pairs)

    mine, ahead = own_picks(emb, pick_rows, owners, block_rows)
    panel = lax.all_to_all(mine, "rows", 0, 0, tiled=True).reshape(owners * rounds, width)

    message = given_first(ahead, panel)
    got = swap_first(message)
    passing, staying = given_rest(emb, panel, block_rows, 1, message)
    next_got = swap_first(passing)
    sent, own = zip(
        kept_products(emb, panel, got, message, block_rows, 0), kept_products(emb, panel, next_got, passing, block_rows, 1)
    )
    quarters = [swap_second(m) for m in sent]
    staying = swap_first(in_order(staying, sent[1]))
    right = update_matrix(sent[0], quarters[0], panel)

    totals = [added([own[0], quarters[0]], []), added([own[1], staying, quarters[1]], [right])]
    near = [swap_second(t) for t in totals]
    theirs = [swap_first(t) for t in totals]
    last = count - 1
    across = []
    for k in range(last):
        near[k] = in_order(near[k], theirs[k])
        across.append(swap_first(near[k]))
    pieces = [(totals[k], 0, k, False, True) for k in range(count)]
    pieces += [(near[k], 0, k, False, False) for k in range(last)]
    out, token = update(emb, right, None, pieces, block_rows, "update_near", True)
    near[last] = in_order(near[last], token)
    across.append(swap_first(near[last]))
    pieces = [(near[last], 0, last, False, False)]
    pieces += [(theirs[k], 0, k, True, True) for k in range(count)]
    pieces += [(across[k], 0, k, True, False) for k in range(last)]
    (out,) = update(emb, right, out, pieces, block_rows, "update_far")
    (out,) = update(emb, right, out, [(across[last], 0, last, True, False)], block_rows, "update_last")
    return out


def solution(mesh):
    return jax.shard_map(
        functools.partial(per_device, owners=mesh.shape["rows"]),
        mesh=mesh,
        in_specs=(P("rows", "cols"), P()),
        out_specs=P("rows", "cols"),
        check_vma=False,
    )
```

```python
import functools

import jax
import jax.numpy as jnp
from jax import lax
from jax.experimental import pallas as pl
from jax.experimental.pallas import tpu as pltpu
from jax.sharding import PartitionSpec as P

HIGH = lax.Precision.HIGHEST
CHUNKS = (512, 512)
VMEM_LIMIT = 16 * 1024 * 1024
F32, BF16 = jnp.float32, jnp.bfloat16


def whole():
    return pl.BlockSpec(memory_space=pltpu.VMEM)


def anywhere():
    return pl.BlockSpec(memory_space=pl.ANY)


def scalars():
    return pl.BlockSpec(memory_space=pltpu.SMEM)


def in_vmem(array):
    return pltpu.with_memory_space_constraint(array, pltpu.VMEM)


def in_hbm(array):
    return pltpu.with_memory_space_constraint(array, pltpu.HBM)


def in_hbm(array):
    return pltpu.with_memory_space_constraint(array, pltpu.HBM)


def call(body, out_shape, in_specs, out_specs, scratch=(), aliases=None, name=None, micros=1.0):
    return pl.pallas_call(
        body,
        out_shape=out_shape,
        in_specs=in_specs,
        out_specs=out_specs,
        scratch_shapes=list(scratch),
        input_output_aliases=aliases or {},
        compiler_params=pltpu.CompilerParams(vmem_limit_bytes=VMEM_LIMIT),
        cost_estimate=pl.CostEstimate(flops=0, bytes_accessed=int(micros * 3.0e6), transcendentals=0),
        name=name,
    )


def first_partner(core, place):
    return place ^ 1 if core == 0 else place ^ 3


def second_partner(core, place):
    return place ^ 3 if core == 0 else place ^ 1


def kept():
    place, odd = lax.axis_index("cols"), lax.rem(lax.axis_index("rows"), 2) == 1
    high, low = place // 2, lax.rem(place, 2)
    gray = lax.rem(high + low, 2)
    return jnp.where(odd, high, gray), jnp.where(odd, low, high), jnp.where(odd, 1 - low, high)


def tile_of(size):
    return max(s for s in range(16, 257, 16) if size % s == 0)


def block_start(half, quarter, block_rows, chunk):
    return (2 * half + quarter) * block_rows + 2 * sum(CHUNKS[:chunk])


def own_picks(emb, pick_rows, copies, block_rows):
    rows, width = emb.shape
    rounds, picks = pick_rows.shape
    tile, size = 16, 2 * CHUNKS[0]

    def body(picks_ref, emb_ref, out_ref, ahead_ref, table, held, sems, table_sem, ahead_sems):
        load = pltpu.make_async_copy(picks_ref, table, table_sem)
        load.start()
        half, _, quarter = kept()
        moves = []
        for j in range(2):
            base = block_start(1 - half, quarter if j else 1 - quarter, block_rows, 0)
            for g in range(2):
                at = g * (size // 2)
                moves.append(
                    pltpu.make_async_copy(
                        emb_ref.at[pl.ds(pl.multiple_of(base + at, 16), size // 2), :],
                        ahead_ref.at[j, pl.ds(at, size // 2), :],
                        ahead_sems.at[2 * j + g],
                    )
                )
        for move in moves:
            move.start()
        load.wait()
        first = lax.axis_index("rows") * rows
        offsets, found = [], []
        for r in range(rounds):
            local = jnp.int32(0)
            for i in range(picks):
                at = table[r, i] - first
                local = local + jnp.where((at >= 0) & (at < rows), at, 0)
            base = pl.multiple_of((local // tile) * tile, tile)
            offsets.append(local - base)
            move = pltpu.make_async_copy(emb_ref.at[pl.ds(base, tile), :], held.at[r], sems.at[r])
            move.start()
            found.append(move)
        for r in range(rounds):
            found[r].wait()
            block = held[r].astype(F32)
            line = lax.broadcasted_iota(jnp.int32, (tile, width), 0)
            row = jnp.sum(jnp.where(line == offsets[r], block, 0.0), axis=0, keepdims=True)
            out_ref[:, r : r + 1, :] = jnp.broadcast_to(row[None], (copies, 1, width))
        for move in moves:
            move.wait()

    return call(
        body,
        [pltpu.VMEM((copies, rounds, width), F32), pltpu.VMEM((2, size, width), BF16)],
        [anywhere(), anywhere()],
        [whole(), whole()],
        [
            pltpu.SMEM((rounds, picks), jnp.int32),
            pltpu.VMEM((rounds, tile, width), BF16),
            pltpu.SemaphoreType.DMA((rounds,)),
            pltpu.SemaphoreType.DMA,
            pltpu.SemaphoreType.DMA((4,)),
        ],
        name="own_picks",
    )(in_hbm(pick_rows), in_hbm(emb))


def paired_panel(panel):
    panel = panel.astype(BF16)
    zero = jnp.zeros_like(panel)
    return jnp.concatenate(
        [jnp.concatenate([panel, zero], axis=1), jnp.concatenate([zero, panel], axis=1)], axis=0
    )


def paired_products(top, bottom, paired):
    both = jnp.concatenate([top, bottom], axis=1)
    return lax.dot_general(both, paired, (((1,), (1,)), ((), ())), preferred_element_type=F32)


def given_first(ahead, panel):
    picks = panel.shape[0]
    size = CHUNKS[0]

    def body(ahead_ref, panel_ref, out_ref):
        panel = panel_ref[...]
        paired = paired_panel(panel)
        low = panel.astype(BF16)
        out_ref[2 * size :, :] = paired_products(low[: picks // 2], low[picks // 2 :], paired)
        for j in range(2):
            out_ref[j * size : (j + 1) * size, :] = paired_products(ahead_ref[j, :size, :], ahead_ref[j, size:, :], paired)

    return call(
        body, pltpu.VMEM((2 * size + picks // 2, 2 * picks), F32), [whole(), whole()], whole(), name="given_first"
    )(in_vmem(ahead), in_vmem(panel))


def quarter_products(emb_ref, start, size, paired):
    start = pl.multiple_of(start, 16)
    return paired_products(emb_ref[pl.ds(start, size), :], emb_ref[pl.ds(start + size, size), :], paired)


def given_rest(emb, panel, block_rows, k, after):
    picks = panel.shape[0]
    size = CHUNKS[k]

    def body(emb_ref, panel_ref, _, pass_ref, own_ref):
        half, _, quarter = kept()
        paired = paired_panel(panel_ref[...])
        pass_ref[...] = quarter_products(emb_ref, block_start(1 - half, 1 - quarter, block_rows, k), size, paired)
        own_ref[...] = quarter_products(emb_ref, block_start(1 - half, quarter, block_rows, k), size, paired)

    return call(
        body,
        [pltpu.VMEM((size, 2 * picks), F32)] * 2,
        [whole(), whole(), anywhere()],
        [whole()] * 2,
        name="given_rest",
    )(emb, in_vmem(panel), after)


def passed_products(emb, panel, got, message, block_rows, k):
    picks = panel.shape[0]
    size = CHUNKS[k]
    extra = picks // 2 if k == 0 else 0

    def body(emb_ref, panel_ref, got_ref, mine_ref, out_ref):
        half, quarter, _ = kept()
        paired = paired_panel(panel_ref[...])
        start = block_start(half, 1 - quarter, block_rows, k)
        out_ref[:size, :] = quarter_products(emb_ref, start, size, paired) + got_ref[:size, :]
        if extra:
            out_ref[size:, :] = got_ref[2 * size :, :] + mine_ref[2 * size :, :]

    return call(
        body, pltpu.VMEM((size + extra, 2 * picks), F32), [whole()] * 4, whole(), name="passed_products"
    )(emb, in_vmem(panel), in_vmem(got), in_vmem(message))


def own_products(emb, panel, got, block_rows, k, after):
    picks = panel.shape[0]
    size = CHUNKS[k]

    def body(emb_ref, panel_ref, got_ref, _, out_ref):
        half, quarter, _ = kept()
        paired = paired_panel(panel_ref[...])
        mine = quarter_products(emb_ref, block_start(half, quarter, block_rows, k), size, paired)
        out_ref[...] = mine + got_ref[size : 2 * size, :] if k == 0 else mine

    return call(
        body, pltpu.VMEM((size, 2 * picks), F32), [whole()] * 3 + [anywhere()], whole(), name="own_products"
    )(emb, in_vmem(panel), in_vmem(got), after)


def added(parts, after):
    shape = parts[0].shape

    def body(*refs):
        total = refs[0][...]
        for ref in refs[1 : len(parts)]:
            total = total + ref[: shape[0], :]
        refs[-1][...] = total

    count = len(parts) + len(after)
    return call(body, pltpu.VMEM(shape, F32), [whole()] * count, whole(), name="added")(
        *[in_vmem(p) for p in parts], *[in_vmem(a) for a in after]
    )


def in_order(value, *after):
    def body(*refs):
        pass

    return call(
        body,
        pltpu.VMEM(value.shape, F32),
        [whole()] * (1 + len(after)),
        whole(),
        aliases={len(after): 0},
        name="in_order",
    )(*[in_vmem(a) for a in after], in_vmem(value))


def split(value):
    high = value.astype(BF16)
    rest = value - high.astype(F32)
    middle = rest.astype(BF16)
    low = (rest - middle.astype(F32)).astype(BF16)
    return high, middle, low


def dot_full(a, b):
    return jnp.dot(a, b, precision=HIGH, preferred_element_type=F32)


def gram_of(sent_ref, got_ref):
    total = sent_ref[CHUNKS[0] :, :] + got_ref[CHUNKS[0] :, :]
    picks = total.shape[1] // 2
    return jnp.concatenate([total[:, :picks], total[:, picks:]], axis=0)


def pivoted(matrix, first_pivot, last_pivot):
    lane = lax.broadcasted_iota(jnp.int32, matrix.shape, 1)
    line = lax.broadcasted_iota(jnp.int32, matrix.shape, 0)
    for k in range(first_pivot, last_pivot, 2):
        first = jnp.broadcast_to(matrix[:, k : k + 1], matrix.shape)
        second = jnp.broadcast_to(matrix[:, k + 1 : k + 2], matrix.shape)
        a, b, d = first[k : k + 1], second[k : k + 1], second[k + 1 : k + 2]
        scale = 1.0 / (a * d - b * b)
        here, there = lane[:1] == k, lane[:1] == k + 1
        top = jnp.where(here, 1.0, jnp.where(there, 0.0, matrix[k : k + 1]))
        bottom = jnp.where(there, 1.0, jnp.where(here, 0.0, matrix[k + 1 : k + 2]))
        row = (d * top - b * bottom) * scale
        next_row = (a * bottom - b * top) * scale
        cleared = jnp.where((lane == k) | (lane == k + 1), 0.0, matrix)
        rest = cleared - first * row - second * next_row
        matrix = jnp.where(line == k, row, jnp.where(line == k + 1, next_row, rest))
    return matrix


def first_pivots(sent, got):
    picks = sent.shape[1] // 2

    def body(sent_ref, got_ref, out_ref):
        out_ref[...] = pivoted(gram_of(sent_ref, got_ref), 0, picks // 2)

    return call(body, pltpu.VMEM((picks, picks), F32), [whole()] * 2, whole(), name="first_pivots")(
        in_vmem(sent), in_vmem(got)
    )


def update_matrix(sent, got, halfway, panel):
    picks, width = panel.shape

    def body(sent_ref, got_ref, halfway_ref, panel_ref, out_ref):
        gram = gram_of(sent_ref, got_ref)
        inverse = pivoted(halfway_ref[...], picks // 2, picks)
        lane = lax.broadcasted_iota(jnp.int32, gram.shape, 1)
        line = lax.broadcasted_iota(jnp.int32, gram.shape, 0)
        eye = jnp.where(lane == line, 1.0, 0.0)
        inverse = inverse + dot_full(inverse, eye - dot_full(gram, inverse))
        high, middle, low = split(dot_full(inverse, panel_ref[...]))
        out_ref[...] = jnp.concatenate([high, high, high, low, middle, middle], axis=0)

    return call(body, pltpu.VMEM((6 * picks, width), BF16), [whole()] * 4, whole(), name="update_matrix")(
        in_vmem(sent), in_vmem(got), in_vmem(halfway), in_vmem(panel)
    )


def update(emb, right, out, pieces, block_rows, name, token=False):
    rows, width = emb.shape
    picks = right.shape[0] // 6
    steps = []
    for n, (_, _, k, *_) in enumerate(pieces):
        size = CHUNKS[k]
        step = tile_of(size)
        steps += [(n, g, t, step) for g in range(2) for t in range(0, size, step)]
    biggest = max(s[3] for s in steps)
    count = len(pieces)

    def body(*refs):
        emb_ref, right_ref = refs[:2]
        staged, sems = refs[-2:]
        out_ref = refs[-4 if token else -3]
        if token:
            refs[-3][...] = jnp.zeros_like(refs[-3])
        half, quarter, partner_quarter = kept()
        right_mat = right_ref[...]
        moves = []
        for i, (n, g, t, step) in enumerate(steps):
            _, first, k, give, keeper = pieces[n]
            size = CHUNKS[k]
            own_half, own_quarter = (1 - half, partner_quarter) if give else (half, quarter)
            start = block_start(own_half, own_quarter if keeper else 1 - own_quarter, block_rows, k)
            base = pl.multiple_of(start + g * size + t, 16)
            got = refs[2 + n][first + t : first + t + step, :]
            lane = lax.broadcasted_iota(jnp.int32, (step, 2 * picks), 1)
            high = got.astype(BF16).astype(F32)
            rest = got - high
            middle = rest.astype(BF16).astype(F32)
            low = rest - middle
            if g == 0:
                first_part = jnp.where(lane < picks, high, pltpu.roll(middle, picks, 1))
                second_part = jnp.where(lane < picks, low, pltpu.roll(high, picks, 1))
            else:
                first_part = jnp.where(lane < picks, pltpu.roll(high, picks, 1), middle)
                second_part = jnp.where(lane < picks, pltpu.roll(low, picks, 1), high)
            first_part = first_part.astype(BF16)
            left = jnp.concatenate([first_part, second_part.astype(BF16), first_part], axis=1)
            taken = jnp.dot(left, right_mat, preferred_element_type=F32)
            staged[i, :step] = emb_ref[pl.ds(base, step), :].astype(F32) - taken
            move = pltpu.make_async_copy(staged.at[i, pl.ds(0, step)], out_ref.at[pl.ds(base, step), :], sems.at[i])
            move.start()
            moves.append(move)
        for move in moves:
            move.wait()

    operands = [emb, in_vmem(right)] + [in_vmem(p[0]) for p in pieces]
    specs = [whole()] * len(operands)
    aliases = None
    if out is not None:
        operands.append(out)
        specs.append(anywhere())
        aliases = {len(operands) - 1: 0}
    return call(
        body,
        [jax.ShapeDtypeStruct((rows, width), F32)] + [pltpu.VMEM((8, 128), F32)] * token,
        specs,
        [anywhere()] + [whole()] * token,
        [pltpu.VMEM((len(steps), biggest, width), F32), pltpu.SemaphoreType.DMA((len(steps),))],
        aliases,
        name=name,
    )(*operands)


def per_device(emb, pick_rows, owners):
    rows, width = emb.shape
    rounds = pick_rows.shape[0]
    block_rows = rows // 4
    count = len(CHUNKS)
    first_pairs = [(r * 4 + c, r * 4 + first_partner(r % 2, c)) for r in range(owners) for c in range(4)]
    second_pairs = [(r * 4 + c, r * 4 + second_partner(r % 2, c)) for r in range(owners) for c in range(4)]

    def swap_first(value):
        return lax.ppermute(value, ("rows", "cols"), first_pairs)

    def swap_second(value):
        return lax.ppermute(value, ("rows", "cols"), second_pairs)

    mine, ahead = own_picks(emb, pick_rows, owners, block_rows)
    panel = lax.all_to_all(mine, "rows", 0, 0, tiled=True).reshape(owners * rounds, width)

    message = given_first(ahead, panel)
    got = swap_first(message)
    passing, staying = given_rest(emb, panel, block_rows, 1, message)
    next_got = swap_first(passing)
    sent = [
        passed_products(emb, panel, got, message, block_rows, 0),
        passed_products(emb, panel, next_got, passing, block_rows, 1),
    ]
    own = [own_products(emb, panel, g, block_rows, k, sent[k]) for k, g in enumerate((got, next_got))]
    staying = swap_first(in_order(staying, own[1]))
    quarters = [swap_second(m) for m in sent]
    halfway = first_pivots(sent[0], quarters[0])
    right = update_matrix(sent[0], quarters[0], halfway, panel)

    totals = [added([own[0], quarters[0]], []), added([own[1], staying, quarters[1]], [halfway])]
    near = [swap_second(t) for t in totals]
    theirs = [swap_first(t) for t in totals]
    last = count - 1
    across = []
    for k in range(last):
        near[k] = in_order(near[k], theirs[k])
        across.append(swap_first(near[k]))
    pieces = [(totals[k], 0, k, False, True) for k in range(count)]
    pieces += [(near[k], 0, k, False, False) for k in range(last)]
    out, token = update(emb, right, None, pieces, block_rows, "update_near", True)
    near[last] = in_order(near[last], token)
    across.append(swap_first(near[last]))
    pieces = [(near[last], 0, last, False, False)]
    pieces += [(theirs[k], 0, k, True, True) for k in range(count)]
    pieces += [(across[k], 0, k, True, False) for k in range(last)]
    (out,) = update(emb, right, out, pieces, block_rows, "update_far")
    (out,) = update(emb, right, out, [(across[last], 0, last, True, False)], block_rows, "update_last")
    return out


def solution(mesh):
    return jax.shard_map(
        functools.partial(per_device, owners=mesh.shape["rows"]),
        mesh=mesh,
        in_specs=(P("rows", "cols"), P()),
        out_specs=P("rows", "cols"),
        check_vma=False,
    )
```
